512 devices in a mesh: row: 32 (over x, y, core), col: 16 (over z).
Axes of the slice: x: 4, y: 4, z: 16, core: 2. Of those that a mesh axis runs over, the one named last changes fastest.
Arguments:
- row_desc: bfloat16 [65536, 1024], P(('row', 'col')), may hold values from -80 to 80
- row_scale: float32 [65536], P('row'), may hold values from 0.3 to 0.9
- col_desc: bfloat16 [32768, 1024], P('col'), may hold values from -80 to 80
- col_scale: bfloat16 [32768], P('col'), may hold values from 0.29882812 to 0.8984375
- probe: bfloat16 [32768, 128], P('col'), may hold values from -5 to 5
- pair_list: int32 [64, 24], P('row'), may hold values from -1 to 31, as said below
Outputs:
- basis_out: float32 [65536, 128], P(('row', 'col'))
- r_factor: float32 [128, 128], replicated
The draws below stay inside these ranges and needn't reach their ends.
Inputs may be any that keep to these rules, and one draw needn't show every extreme that they name: Each row of pair_list holds distinct column block numbers first and -1 in the remaining slots; each row block lists between 16 and 24 blocks, and row block 0 lists 24. Some column blocks are listed far more often than others.
All inputs are finite; a program needn't handle non-finite values.
Results may differ from the reference program's by a relative error of at most 0.0061.
Values may be sent and summed in bfloat16 or wider, within the bound.
A program may use at most 64 MiB of HBM per device.

```python
import math
import jax
import jax.numpy as jnp
from jax import lax

D = 1024
PROBES = 128
BLK = 1024
NRB = 64
NCB = 32
ROWS = 65536
COLS = 32768
MAXP = 24


def shared_parts(key):
    centre_count = max(COLS // 128, 4)
    centres = jax.random.truncated_normal(jax.random.fold_in(key, 101), -4.0, 4.0, (centre_count, D), jnp.float32)
    return centres


def assemble(key, total, centres, noise):
    key_id, key_spread, key_size = jax.random.split(key, 3)
    member = jax.random.randint(key_id, (total,), 0, centres.shape[0])
    spread = jax.random.uniform(key_spread, (total, 1), jnp.float32, 0.3, 1.0)
    magnitude = jnp.exp(jax.random.uniform(key_size, (total, 1), jnp.float32, 0.0, math.log(10.0)))
    picked = jnp.take(centres, member, axis=0)
    return (magnitude * (picked + spread * noise)).astype(jnp.bfloat16)


def draw_row_desc(key, part):
    centres = shared_parts(key)
    key = jax.random.fold_in(key, 3)
    key_noise, key_rest = jax.random.split(key)
    noise = jax.random.truncated_normal(key_noise, -4.0, 4.0, (ROWS, D), jnp.float32)
    return assemble(key_rest, ROWS, centres, noise)


def draw_col_desc(key, part):
    centres = shared_parts(key)
    key = jax.random.fold_in(key, 5)
    key_noise, key_rest = jax.random.split(key)
    noise = jax.random.truncated_normal(key_noise, -4.0, 4.0, (COLS, D), jnp.float32)
    return assemble(key_rest, COLS, centres, noise)


def draw_pair_list(key, part):
    key = jax.random.fold_in(key, 11)
    key_pop, key_noise, key_count = jax.random.split(key, 3)
    popular = jnp.left_shift(jnp.ones((NCB,), jnp.int32), jax.random.randint(key_pop, (NCB,), 0, 4))
    noise = jax.random.randint(key_noise, (NRB, NCB), 0, 4096)
    scores = noise * popular[None, :] * NCB + jnp.arange(NCB, dtype=jnp.int32)[None, :]
    values, chosen = lax.top_k(scores, MAXP)
    counts = jax.random.randint(key_count, (NRB,), NCB // 2, MAXP + 1)
    counts = counts.at[0].set(MAXP)
    slots = jnp.arange(MAXP, dtype=jnp.int32)
    return jnp.where(slots[None, :] < counts[:, None], chosen, -1).astype(jnp.int32)


def steps_of(own_key, shape, pieces, low, largest):
    def one(axis_at, shards_of):
        heights = jax.random.uniform(jax.random.fold_in(jax.random.fold_in(own_key, 6), axis_at), (shards_of,), jnp.float32, low / len(pieces), largest / len(pieces))
        return jnp.repeat(jnp.exp(heights), shape[axis_at] // shards_of).reshape((-1,) + (1,) * (len(shape) - axis_at - 1))

    gain = one(*pieces[0])
    for cut in pieces[1:]:
        gain = gain * one(*cut)
    return gain


def gaussian(own_key, shape, width, reach, cuts=(), kind=jnp.bfloat16):
    gain = steps_of(own_key, shape, cuts, -0.22, 0.18) if cuts else 1.0
    array = jax.random.normal(own_key, shape, jnp.float32) * width * gain
    return jnp.minimum(jnp.maximum(array, -reach), reach).astype(kind)


def setup_inputs(seed: int = 0) -> dict:
    keys = jax.random.split(jax.random.key(seed), 7)
    row_desc = draw_row_desc(jax.random.fold_in(keys[6], 71), 0)
    row_scale = jnp.clip(jnp.exp(math.log(0.9) - 1.0986122 * jax.random.uniform(keys[1], (ROWS,), jnp.float32) ** steps_of(keys[1], (ROWS,), ((0, 32),), -0.2, 0.2)), 0.3, 0.9)
    col_desc = draw_col_desc(jax.random.fold_in(keys[6], 71), 0)
    col_scale = jnp.clip(jnp.exp(math.log(0.8984375) - 1.1007886 * jax.random.uniform(keys[3], (COLS,), jnp.float32) ** steps_of(keys[3], (COLS,), ((0, 16),), -0.2, 0.2)), 0.29882812, 0.8984375).astype(jnp.bfloat16)
    probe = gaussian(keys[4], (COLS, PROBES), 1.0, 5.0, ((0, 16),))
    pair_list = draw_pair_list(jax.random.fold_in(keys[6], 71), 0)
    return {"row_desc": row_desc, "row_scale": row_scale, "col_desc": col_desc, "col_scale": col_scale, "probe": probe, "pair_list": pair_list}


def unit_rows(descriptors):
    widened = descriptors.astype(jnp.float32)
    total = lax.optimization_barrier(jnp.sum(widened * widened, axis=1, keepdims=True))
    return (widened * lax.rsqrt(total + 1e-06)).astype(jnp.bfloat16)

def tile_sketch(row_tile, row_band, col_tile, col_band, probe_tile):
    cosine = jnp.dot(row_tile.astype(jnp.float32), col_tile.T.astype(jnp.float32), preferred_element_type=jnp.float32)
    affinity = jnp.exp((2.0 * cosine - 2.0) / (row_band[:, None] * col_band[None, :])).astype(jnp.bfloat16)
    return jnp.dot(affinity.astype(jnp.float32), probe_tile.astype(jnp.float32), preferred_element_type=jnp.float32)

def reference(row_desc, row_scale, col_desc, col_scale, probe, pair_list):
    row_unit = unit_rows(row_desc)
    col_unit = unit_rows(col_desc)
    col_band = col_scale.astype(jnp.float32)

    def one_block(b):
        offset = (b * BLK).astype(jnp.int32)
        row_tile = lax.dynamic_slice_in_dim(row_unit, offset, BLK, 0)
        row_band = lax.dynamic_slice_in_dim(row_scale, offset, BLK, 0)

        def one_slot(s, running):
            target = pair_list[b, s]

            def add_tile(current):
                col_start = (jnp.maximum(target, 0) * BLK).astype(jnp.int32)
                col_tile = lax.dynamic_slice_in_dim(col_unit, col_start, BLK, 0)
                band_tile = lax.dynamic_slice_in_dim(col_band, col_start, BLK, 0)
                probe_tile = lax.dynamic_slice_in_dim(probe, col_start, BLK, 0)
                return current + tile_sketch(row_tile, row_band, col_tile, band_tile, probe_tile)

            def keep_tile(current):
                return current
            return lax.cond(target >= 0, add_tile, keep_tile, running)
        return lax.fori_loop(0, MAXP, one_slot, jnp.zeros((BLK, PROBES), jnp.float32))
    sketch = lax.map(one_block, jnp.arange(NRB, dtype=jnp.int32)).reshape(ROWS, PROBES)
    gram_sum = jnp.dot(sketch.T.astype(jnp.float32), sketch.astype(jnp.float32), precision=lax.Precision.HIGHEST, preferred_element_type=jnp.float32) / ROWS
    factor_low = jnp.linalg.cholesky(gram_sum)
    basis_out = jax.scipy.linalg.solve_triangular(factor_low, sketch.T, lower=True).T
    return (basis_out, factor_low.T)
```

```python
import functools

import jax
import jax.numpy as jnp
from jax import lax
from jax.experimental import pallas as pl
from jax.experimental.pallas import tpu as pltpu
from jax.sharding import PartitionSpec as P


RING = 16
OWN, FAR = 14, 15
SIDE = 128
HALF = 64
BLK = 1024
MESH = pl.DeviceIdType.MESH
LOG2E = 1.4426950408889634
F32 = jnp.float32
BF16 = jnp.bfloat16
RINGS = 3


def offset_of(slot):
    if slot == OWN:
        return 0
    if slot == FAR:
        return 8
    distance = slot // 2 + 1
    return -distance if slot % 2 == 0 else distance


def slot_of_offset(offset):
    offset %= RING
    if offset == 0:
        return OWN
    if offset == 8:
        return FAR
    return 2 * (RING - offset - 1) if offset > 8 else 2 * (offset - 1) + 1


def unit_rows(block):
    wide = block.astype(F32)
    total = jnp.sum(wide * wide, axis=1, keepdims=True)
    return (wide * lax.rsqrt(total + 1e-06)).astype(BF16)


def sketch_kernel(
    row_ref, rscale_ref, col_ref, cscale_ref, probe_ref, pair_ref,
    sketch_ref, gram_ref,
    rows, cols, stage, raux, bvec, mstack, cmat, ascale, acc, landed, gsrc, g1, g2, g3,
    local_sem, ring_send, ring_recv, sib_send, sib_recv, raux_send, raux_recv, caux_send, caux_recv,
    red_send, red_recv, d1_send, d1_recv, d2_send, d2_recv, d3_send, d3_recv,
):
    r = lax.axis_index("row")
    z = lax.axis_index("col")
    core = lax.rem(r, 2)
    p = r // 2
    x = p // 4
    y = lax.rem(p, 4)
    diag = lax.rem(x + y, 4)
    pos = (4 * x + diag, 4 * y + diag)

    def chip_at(ring, place):
        place = lax.rem(place + 2 * RING, RING)
        a = place // 4
        b = lax.rem(place - a + 8, 4)
        return 4 * a + b if ring == 0 else 4 * b + a

    def device_at(ring, offset):
        if ring == 2:
            return (r, lax.rem(z + offset + RING, RING))
        return (2 * chip_at(ring, pos[ring] + offset) + core, z)

    sibling = (2 * p + 1 - core, z)

    barrier = pltpu.get_barrier_semaphore()

    def greet_plane(i, carry):
        pl.semaphore_signal(
            barrier, inc=1, device_id=(lax.rem(r + i, 32), z), device_id_type=MESH
        )
        return carry

    def greet_ring(i, carry):
        pl.semaphore_signal(
            barrier, inc=1, device_id=(r, lax.rem(z + i, RING)), device_id_type=MESH
        )
        return carry

    lax.fori_loop(1, 32, greet_plane, 0)
    lax.fori_loop(1, RING, greet_ring, 0)

    start = pl.multiple_of(p * SIDE, SIDE)
    col_copy = pltpu.make_async_copy(col_ref.at[pl.ds(start, SIDE)], stage, local_sem.at[0])
    probe_copy = pltpu.make_async_copy(
        probe_ref.at[pl.ds(start, SIDE)], cols.at[OWN, :, pl.ds(1024, SIDE)], local_sem.at[1]
    )
    col_copy.start()
    probe_copy.start()
    rows[OWN] = unit_rows(row_ref[...])
    lane = lax.broadcasted_iota(jnp.int32, (1, SIDE), 1)
    block_row = z // 8
    mask = jnp.zeros((1, SIDE), F32)
    for s in range(pair_ref.shape[1]):
        mask = jnp.where(lane == pair_ref[block_row, s], 1.0, mask)
    raux[p, 0:1, :] = (2.0 * LOG2E) / rscale_ref[pl.ds(z, 1), :]
    raux[p, 1:2, :] = mask
    bvec[OWN] = 1.0 / cscale_ref[pl.ds(p, 1), :]
    col_copy.wait()
    cols[OWN, :, :1024] = unit_rows(stage[...])
    probe_copy.wait()
    pl.semaphore_wait(barrier, 46)

    half = pl.ds(pl.multiple_of(core * HALF, HALF), HALF)

    def ring_copy(ring, way, step):
        source = OWN if step == 1 else 2 * (step - 2) + way
        target = FAR if step == 8 else 2 * (step - 1) + way
        low, count = (0, HALF) if step < 8 else (way * HALF // 2, HALF // 2)
        if ring == 2:
            part = pl.ds(pl.multiple_of(core * HALF + low, HALF // 2), count)
            buffer = cols
        else:
            part = pl.ds(ring * HALF + low, count)
            buffer = rows
        return pltpu.make_async_remote_copy(
            src_ref=buffer.at[source, part],
            dst_ref=buffer.at[target, part],
            send_sem=ring_send.at[ring, way, step - 1],
            recv_sem=ring_recv.at[ring, way, step - 1],
            device_id=device_at(ring, 1 - 2 * way),
            device_id_type=MESH,
        )

    def sibling_copy(step):
        first, count = (2 * (step - 1), 2) if step < 8 else (FAR, 1)
        return pltpu.make_async_remote_copy(
            src_ref=cols.at[pl.ds(first, count), half],
            dst_ref=cols.at[pl.ds(first, count), half],
            send_sem=sib_send.at[step - 1],
            recv_sem=sib_recv.at[step - 1],
            device_id=sibling,
            device_id_type=MESH,
        )

    sent = {}
    for ring in range(RINGS):
        for way in range(2):
            sent[ring, way, 1] = ring_copy(ring, way, 1)
            sent[ring, way, 1].start()

    def raux_copy(i):
        other = lax.rem(p + i, RING)
        return pltpu.make_async_remote_copy(
            src_ref=raux.at[p],
            dst_ref=raux.at[p],
            send_sem=raux_send.at[i],
            recv_sem=raux_recv.at[p],
            device_id=(2 * other + core, z),
            device_id_type=MESH,
        )

    def raux_arrival(i):
        other = lax.rem(p + i, RING)
        return pltpu.make_async_remote_copy(
            src_ref=raux.at[other],
            dst_ref=raux.at[other],
            send_sem=raux_send.at[i],
            recv_sem=raux_recv.at[other],
            device_id=(2 * other + core, z),
            device_id_type=MESH,
        )

    def caux_copy(offset):
        target = slot_of_offset(-offset)
        return pltpu.make_async_remote_copy(
            src_ref=bvec.at[OWN],
            dst_ref=bvec.at[target],
            send_sem=caux_send.at[target],
            recv_sem=caux_recv.at[target],
            device_id=device_at(2, offset),
            device_id_type=MESH,
        )

    def each(count, act):
        def body(i, carry):
            act(i)
            return carry

        lax.fori_loop(1, count, body, 0)

    each(RING, lambda i: raux_copy(i).start())
    caux = [caux_copy(offset) for offset in range(1, RING)]
    for copy in caux:
        copy.start()

    def prepare():
        each(RING, lambda i: raux_arrival(i).wait_recv())
        for copy in caux:
            copy.wait_recv()
        eye = lax.broadcasted_iota(jnp.int32, (SIDE, SIDE), 0) == lax.broadcasted_iota(
            jnp.int32, (SIDE, SIDE), 1
        )
        for slot in range(RING):
            first = raux[chip_at(0, pos[0] + offset_of(slot))]
            second = raux[chip_at(1, pos[1] + offset_of(slot))]
            mstack[2 * slot : 2 * slot + 1, :] = first[1:2]
            mstack[2 * slot + 1 : 2 * slot + 2, :] = second[1:2]
            scale = jnp.where(lane < HALF, first[0:1], second[0:1])
            column = jnp.sum(jnp.where(eye, scale, 0.0), axis=1, keepdims=True)
            ascale[slot * SIDE : (slot + 1) * SIDE, :] = jnp.broadcast_to(column, (SIDE, SIDE))
        width = RING * SIDE
        slot_at = lax.broadcasted_iota(jnp.int32, (SIDE, width), 1) // SIDE
        step_at = slot_at // 2 + 1
        shift = jnp.where(slot_at == 2 * (step_at - 1), -step_at, step_at)
        shift = jnp.where(slot_at == OWN, 0, shift)
        shift = jnp.where(slot_at == FAR, 8, shift)
        plane_at = (shift + z + RING) & (RING - 1)
        wanted = lax.broadcasted_iota(jnp.int32, (SIDE, width), 0) == 2 * plane_at + p // 8
        chosen = jnp.dot(
            mstack[...].astype(BF16), wanted.astype(F32).astype(BF16), preferred_element_type=F32
        )
        cmat[...] = (1.0 - chosen) * 1e30 + 1.0

    def tile(r0, m, c0, n):
        lhs = rows[r0 : r0 + m].reshape(m * SIDE, 1024)
        rhs = cols[c0 : c0 + n, :, :1024].reshape(n * SIDE, 1024)
        cosine = lax.dot_general(
            lhs, rhs, (((1,), (1,)), ((), ())), preferred_element_type=F32
        )
        inverse = jnp.concatenate([bvec[c] for c in range(c0, c0 + n)], axis=1)
        parts = []
        for piece in range(2 * m):
            at = 2 * r0 + piece
            shifted = (
                cosine[piece * HALF : (piece + 1) * HALF]
                - cmat[at : at + 1, c0 * SIDE : (c0 + n) * SIDE]
            )
            power = shifted * inverse * ascale[at * HALF : (at + 1) * HALF, :1]
            parts.append(jnp.exp2(power).astype(BF16))
        affinity = jnp.concatenate(parts, axis=0)
        probes = cols[c0 : c0 + n, :, 1024:].reshape(n * SIDE, SIDE)
        return jnp.dot(affinity, probes, preferred_element_type=F32).reshape(m, SIDE, SIDE)

    def add_rows(q):
        acc[2 * q : 2 * q + 2] = tile(2 * q, 2, 0, 2 * q + 2)

    def add_cols(low, high, q):
        if high > low:
            span = slice(2 * low, 2 * high)
            acc[span] = acc[span] + tile(2 * low, 2 * (high - low), 2 * q, 2)

    siblings = {}
    for step in range(1, 9):
        if step == 2:
            prepare()
        if step >= 2:
            siblings[step - 1].wait_recv()
            add_rows(step - 2)
            add_cols(0, step - 2, step - 2)
        for ring in range(RINGS):
            for way in range(2):
                sent[ring, way, step].wait_recv()
                if step < 8:
                    sent[ring, way, step + 1] = ring_copy(ring, way, step + 1)
                    sent[ring, way, step + 1].start()
        siblings[step] = sibling_copy(step)
        siblings[step].start()
    siblings[8].wait_recv()

    reduces = []

    def send_back(slot):
        for ring in range(2):
            index = slot if slot < OWN else OWN
            part = pl.ds(ring * HALF, HALF)
            copy = pltpu.make_async_remote_copy(
                src_ref=acc.at[slot, part],
                dst_ref=landed.at[index, part],
                send_sem=red_send.at[index, ring],
                recv_sem=red_recv.at[index, ring],
                device_id=device_at(ring, offset_of(slot)),
                device_id_type=MESH,
            )
            copy.start()
            reduces.append(copy)

    add_rows(7)
    send_back(FAR)
    add_cols(0, 4, 7)
    for slot in range(8):
        send_back(slot)
    add_cols(4, 7, 7)
    for slot in range(8, OWN):
        send_back(slot)
    for copy in reduces:
        copy.wait_recv()
    total = acc[OWN]
    for index in range(RING - 1):
        total = total + landed[index]
    sketch_ref[...] = total

    gram = lax.dot_general(
        total, total, (((0,), (0,)), ((), ())),
        precision=lax.Precision.HIGHEST, preferred_element_type=F32,
    )
    gsrc[...] = gram.reshape(RING, 8, SIDE)

    def d1_copy(i):
        other = lax.rem(r + i, 32)
        return pltpu.make_async_remote_copy(
            src_ref=gsrc.at[other // 2],
            dst_ref=g1.at[r],
            send_sem=d1_send.at[i],
            recv_sem=d1_recv.at[r],
            device_id=(other, z),
            device_id_type=MESH,
        )

    def d1_arrival(i):
        other = lax.rem(r + i, 32)
        return pltpu.make_async_remote_copy(
            src_ref=gsrc.at[0],
            dst_ref=g1.at[other],
            send_sem=d1_send.at[i],
            recv_sem=d1_recv.at[other],
            device_id=(other, z),
            device_id_type=MESH,
        )

    each(32, lambda i: d1_copy(i).start())
    g1[r] = gsrc[p]
    each(32, lambda i: d1_arrival(i).wait_recv())
    g2[z] = jnp.sum(g1[...], axis=0)

    def d2_copy(i, mine):
        other = lax.rem(z + i, RING)
        at = z if mine else other
        return pltpu.make_async_remote_copy(
            src_ref=g2.at[at],
            dst_ref=g2.at[at],
            send_sem=d2_send.at[i],
            recv_sem=d2_recv.at[at],
            device_id=(r, other),
            device_id_type=MESH,
        )

    each(RING, lambda i: d2_copy(i, True).start())
    each(RING, lambda i: d2_copy(i, False).wait_recv())
    g3[p] = jnp.sum(g2[...], axis=0)

    def d3_copy(i, mine):
        other = lax.rem(p + i, RING)
        at = p if mine else other
        return pltpu.make_async_remote_copy(
            src_ref=g3.at[at],
            dst_ref=g3.at[at],
            send_sem=d3_send.at[i],
            recv_sem=d3_recv.at[at],
            device_id=(2 * other + core, z),
            device_id_type=MESH,
        )

    each(RING, lambda i: d3_copy(i, True).start())
    each(RING, lambda i: d3_copy(i, False).wait_recv())
    gram_ref[...] = g3[...].reshape(SIDE, SIDE) * (1.0 / 65536.0)

    for copy in sent.values():
        copy.wait_send()
    for copy in siblings.values():
        copy.wait_send()
    for copy in reduces:
        copy.wait_send()
    for copy in caux:
        copy.wait_send()
    each(RING, lambda i: raux_copy(i).wait_send())
    each(32, lambda i: d1_copy(i).wait_send())
    each(RING, lambda i: d2_copy(i, True).wait_send())
    each(RING, lambda i: d3_copy(i, True).wait_send())


def sketch_and_gram(row_desc, row_scale, col_desc, col_scale, probe, pair_list):
    vmem = pl.BlockSpec(memory_space=pltpu.VMEM)
    hbm = pl.BlockSpec(memory_space=pl.ANY)
    smem = pl.BlockSpec(memory_space=pltpu.SMEM)
    dma = pltpu.SemaphoreType.DMA
    square = jax.ShapeDtypeStruct((SIDE, SIDE), F32)
    return pl.pallas_call(
        sketch_kernel,
        name="sketch_and_gram",
        out_shape=(square, square),
        in_specs=[vmem, vmem, hbm, vmem, hbm, smem],
        out_specs=(vmem, vmem),
        scratch_shapes=[
            pltpu.VMEM((RING, SIDE, 1024), BF16),
            pltpu.VMEM((RING, SIDE, 1024 + SIDE), BF16),
            pltpu.VMEM((SIDE, 1024), BF16),
            pltpu.VMEM((RING, 2, SIDE), F32),
            pltpu.VMEM((RING, 1, SIDE), F32),
            pltpu.VMEM((2 * RING, SIDE), F32),
            pltpu.VMEM((2 * RING, RING * SIDE), F32),
            pltpu.VMEM((RING * SIDE, SIDE), F32),
            pltpu.VMEM((RING, SIDE, SIDE), F32),
            pltpu.VMEM((RING - 1, SIDE, SIDE), F32),
            pltpu.VMEM((RING, 8, SIDE), F32),
            pltpu.VMEM((32, 8, SIDE), F32),
            pltpu.VMEM((RING, 8, SIDE), F32),
            pltpu.VMEM((RING, 8, SIDE), F32),
            dma((2,)),
            dma((RINGS, 2, 8)),
            dma((RINGS, 2, 8)),
            dma((8,)),
            dma((8,)),
            dma((RING,)),
            dma((RING,)),
            dma((RING,)),
            dma((RING,)),
            dma((RING - 1, 2)),
            dma((RING - 1, 2)),
            dma((32,)),
            dma((32,)),
            dma((RING,)),
            dma((RING,)),
            dma((RING,)),
            dma((RING,)),
        ],
        compiler_params=pltpu.CompilerParams(
            collective_id=0, has_side_effects=True, vmem_limit_bytes=56 << 20
        ),
    )(
        row_desc,
        row_scale.reshape(RING, SIDE),
        col_desc,
        col_scale.astype(F32).reshape(RING, SIDE),
        probe,
        pair_list,
    )


def shards(row_desc, row_scale, col_desc, col_scale, probe, pair_list):
    sketch, gram = sketch_and_gram(row_desc, row_scale, col_desc, col_scale, probe, pair_list)
    factor_low = jnp.linalg.cholesky(gram)
    basis_out = jax.scipy.linalg.solve_triangular(factor_low, sketch.T, lower=True).T
    return (basis_out, factor_low.T)


def solution(mesh):
    return jax.shard_map(
        shards,
        mesh=mesh,
        in_specs=(
            P(("row", "col"), None),
            P("row"),
            P("col", None),
            P("col"),
            P("col", None),
            P("row", None),
        ),
        out_specs=(P(("row", "col"), None), P()),
        check_vma=False,
    )
```

```python
import functools

import jax
import jax.numpy as jnp
from jax import lax
from jax.experimental import pallas as pl
from jax.experimental.pallas import tpu as pltpu
from jax.sharding import PartitionSpec as P


RING = 16
OWN, FAR = 14, 15
SIDE = 128
HALF = 64
QUARTER = 32
PANEL = 16
MESH = pl.DeviceIdType.MESH
LOG2E = 1.4426950408889634
F32 = jnp.float32
BF16 = jnp.bfloat16
RINGS = 3


def offset_of(slot):
    if slot == OWN:
        return 0
    if slot == FAR:
        return 8
    distance = slot // 2 + 1
    return -distance if slot % 2 == 0 else distance


def slot_of_offset(offset):
    offset %= RING
    if offset == 0:
        return OWN
    if offset == 8:
        return FAR
    return 2 * (RING - offset - 1) if offset > 8 else 2 * (offset - 1) + 1


def unit_rows(block):
    wide = block.astype(F32)
    total = jnp.sum(wide * wide, axis=1, keepdims=True)
    return (wide * lax.rsqrt(total + 1e-06)).astype(BF16)


def sketch_kernel(
    row_hbm, rscale_hbm, col_hbm, cscale_hbm, probe_hbm, pair_hbm,
    sketch_ref, gram_ref,
    rscale, cscale, pairs, wide, rows, cols, stage, raux, bvec, mstack, cmat, ascale, acc, leaving, landed, gsrc, g1, g2, g3,
    local_sem, ring_send, ring_recv, sib_send, sib_recv, raux_send, raux_recv, caux_send, caux_recv,
    red_send, red_recv, d1_send, d1_recv, d2_send, d2_recv, d3_send, d3_recv,
):
    r = lax.axis_index("row")
    z = lax.axis_index("col")
    core = lax.rem(r, 2)
    p = r // 2
    x = p // 4
    y = lax.rem(p, 4)
    diag = lax.rem(x + y, 4)
    pos = (4 * x + diag, 4 * y + diag)

    def chip_at(ring, place):
        place = lax.rem(place + 2 * RING, RING)
        a = place // 4
        b = lax.rem(place - a + 8, 4)
        return 4 * a + b if ring == 0 else 4 * b + a

    def device_at(ring, offset):
        if ring == 2:
            return (r, lax.rem(z + offset + RING, RING))
        return (2 * chip_at(ring, pos[ring] + offset) + core, z)

    sibling = (2 * p + 1 - core, z)

    barrier = pltpu.get_barrier_semaphore()

    def greet_plane(i, carry):
        pl.semaphore_signal(
            barrier, inc=1, device_id=(lax.rem(r + i, 32), z), device_id_type=MESH
        )
        return carry

    def greet_ring(i, carry):
        pl.semaphore_signal(
            barrier, inc=1, device_id=(r, lax.rem(z + i, RING)), device_id_type=MESH
        )
        return carry

    start = pl.multiple_of(p * SIDE, SIDE)
    own = [
        (row_hbm, stage.at[0]),
        (col_hbm.at[pl.ds(start, SIDE)], stage.at[1]),
        (rscale_hbm, rscale),
        (cscale_hbm, cscale),
        (pair_hbm, pairs),
        (probe_hbm.at[pl.ds(start, SIDE)], cols.at[OWN, :, pl.ds(1024, SIDE)]),
    ]
    own = [pltpu.make_async_copy(a, b, local_sem.at[i]) for i, (a, b) in enumerate(own)]
    for copy in own:
        copy.start()
    lax.fori_loop(1, 32, greet_plane, 0)
    lax.fori_loop(1, RING, greet_ring, 0)
    own[0].wait()
    rows[OWN] = unit_rows(stage[0])
    own[1].wait()
    cols[OWN, :, :1024] = unit_rows(stage[1])
    for copy in own[2:]:
        copy.wait()
    lane = lax.broadcasted_iota(jnp.int32, (1, SIDE), 1)
    block_row = z // 8
    mask = jnp.zeros((1, SIDE), F32)
    for s in range(pairs.shape[1]):
        mask = jnp.where(lane == pairs[block_row, s], 1.0, mask)
    raux[p, 0:1, :] = (2.0 * LOG2E) / rscale[pl.ds(z, 1), :]
    raux[p, 1:2, :] = mask
    wide[...] = cscale[...].astype(F32).reshape(RING, SIDE)
    bvec[OWN] = 1.0 / wide[pl.ds(p, 1), :]
    pl.semaphore_wait(barrier, 46)

    half = pl.ds(pl.multiple_of(core * HALF, HALF), HALF)

    def ring_copy(ring, way, step, sub):
        source = OWN if step == 1 else 2 * (step - 2) + way
        target = FAR if step == 8 else 2 * (step - 1) + way
        low = sub * QUARTER
        if ring == 2:
            part = pl.ds(pl.multiple_of(core * HALF + low, QUARTER), QUARTER)
            buffer = cols
        else:
            part = pl.ds(ring * HALF + low, QUARTER)
            buffer = rows
        return pltpu.make_async_remote_copy(
            src_ref=buffer.at[source, part],
            dst_ref=buffer.at[target, part],
            send_sem=ring_send.at[ring, way, step - 1, sub],
            recv_sem=ring_recv.at[ring, way, step - 1, sub],
            device_id=device_at(ring, 1 - 2 * way),
            device_id_type=MESH,
        )

    def sibling_copy(step):
        first, count = (2 * (step - 1), 2) if step < 8 else (FAR, 1)
        return pltpu.make_async_remote_copy(
            src_ref=cols.at[pl.ds(first, count), half],
            dst_ref=cols.at[pl.ds(first, count), half],
            send_sem=sib_send.at[step - 1],
            recv_sem=sib_recv.at[step - 1],
            device_id=sibling,
            device_id_type=MESH,
        )

    sent = {}

    def pass_on(ring, way, step, sub):
        if step < 8 or sub == way:
            sent[ring, way, step, sub] = ring_copy(ring, way, step, sub)
            sent[ring, way, step, sub].start()

    for sub in range(2):
        for ring in range(RINGS):
            for way in range(2):
                pass_on(ring, way, 1, sub)

    def raux_copy(i):
        other = lax.rem(p + i, RING)
        return pltpu.make_async_remote_copy(
            src_ref=raux.at[p],
            dst_ref=raux.at[p],
            send_sem=raux_send.at[i],
            recv_sem=raux_recv.at[p],
            device_id=(2 * other + core, z),
            device_id_type=MESH,
        )

    def raux_arrival(i):
        other = lax.rem(p + i, RING)
        return pltpu.make_async_remote_copy(
            src_ref=raux.at[other],
            dst_ref=raux.at[other],
            send_sem=raux_send.at[i],
            recv_sem=raux_recv.at[other],
            device_id=(2 * other + core, z),
            device_id_type=MESH,
        )

    def caux_copy(offset):
        target = slot_of_offset(-offset)
        return pltpu.make_async_remote_copy(
            src_ref=bvec.at[OWN],
            dst_ref=bvec.at[target],
            send_sem=caux_send.at[target],
            recv_sem=caux_recv.at[target],
            device_id=device_at(2, offset),
            device_id_type=MESH,
        )

    def each(count, act):
        def body(i, carry):
            act(i)
            return carry

        lax.fori_loop(1, count, body, 0)

    each(RING, lambda i: raux_copy(i).start())
    caux = [caux_copy(offset) for offset in range(1, RING)]
    for copy in caux:
        copy.start()

    def prepare():
        each(RING, lambda i: raux_arrival(i).wait_recv())
        for copy in caux:
            copy.wait_recv()
        eye = lax.broadcasted_iota(jnp.int32, (SIDE, SIDE), 0) == lax.broadcasted_iota(
            jnp.int32, (SIDE, SIDE), 1
        )
        for slot in range(RING):
            first = raux[chip_at(0, pos[0] + offset_of(slot))]
            second = raux[chip_at(1, pos[1] + offset_of(slot))]
            mstack[2 * slot : 2 * slot + 1, :] = first[1:2]
            mstack[2 * slot + 1 : 2 * slot + 2, :] = second[1:2]
            scale = jnp.where(lane < HALF, first[0:1], second[0:1])
            column = jnp.sum(jnp.where(eye, scale, 0.0), axis=1, keepdims=True)
            ascale[slot * SIDE : (slot + 1) * SIDE, :] = jnp.broadcast_to(column, (SIDE, SIDE))
        width = RING * SIDE
        slot_at = lax.broadcasted_iota(jnp.int32, (SIDE, width), 1) // SIDE
        step_at = slot_at // 2 + 1
        shift = jnp.where(slot_at == 2 * (step_at - 1), -step_at, step_at)
        shift = jnp.where(slot_at == OWN, 0, shift)
        shift = jnp.where(slot_at == FAR, 8, shift)
        plane_at = (shift + z + RING) & (RING - 1)
        wanted = lax.broadcasted_iota(jnp.int32, (SIDE, width), 0) == 2 * plane_at + p // 8
        chosen = jnp.dot(
            mstack[...].astype(BF16), wanted.astype(F32).astype(BF16), preferred_element_type=F32
        )
        cmat[...] = (1.0 - chosen) * 1e30 + 1.0

    def tile(r0, m, c0, n):
        lhs = rows[r0 : r0 + m].reshape(m * SIDE, 1024)
        rhs = cols[c0 : c0 + n, :, :1024].reshape(n * SIDE, 1024)
        cosine = lax.dot_general(
            lhs, rhs, (((1,), (1,)), ((), ())), preferred_element_type=F32
        )
        inverse = jnp.concatenate([bvec[c] for c in range(c0, c0 + n)], axis=1)
        parts = []
        for piece in range(2 * m):
            at = 2 * r0 + piece
            shifted = (
                cosine[piece * HALF : (piece + 1) * HALF]
                - cmat[at : at + 1, c0 * SIDE : (c0 + n) * SIDE]
            )
            power = shifted * inverse * ascale[at * HALF : (at + 1) * HALF, :1]
            parts.append(jnp.exp2(power).astype(BF16))
        affinity = jnp.concatenate(parts, axis=0)
        probes = cols[c0 : c0 + n, :, 1024:].reshape(n * SIDE, SIDE)
        return jnp.dot(affinity, probes, preferred_element_type=F32).reshape(m, SIDE, SIDE)

    def add_rows(q):
        acc[2 * q : 2 * q + 2] = tile(2 * q, 2, 0, 2 * q + 2)

    def add_cols(low, high, q):
        if high > low:
            span = slice(2 * low, 2 * high)
            acc[span] = acc[span] + tile(2 * low, 2 * (high - low), 2 * q, 2)

    def take(step, sub):
        for ring in range(RINGS):
            for way in range(2):
                if (ring, way, step, sub) in sent:
                    sent[ring, way, step, sub].wait_recv()
                    if step < 8:
                        pass_on(ring, way, step + 1, sub)

    siblings = {}
    for step in range(1, 9):
        take(step, 0)
        if step >= 3:
            siblings[step - 1].wait_recv()
            if step == 3:
                add_rows(0)
            add_rows(step - 2)
        take(step, 1)
        siblings[step] = sibling_copy(step)
        siblings[step].start()
        if step == 2:
            siblings[1].wait_recv()
            prepare()
        if step >= 3:
            add_cols(0, step - 2, step - 2)
    siblings[8].wait_recv()

    reduces = []

    def send_back(slot):
        index = slot if slot < OWN else OWN
        leaving[index] = acc[slot].astype(BF16)
        for ring in range(2):
            part = pl.ds(ring * HALF, HALF)
            copy = pltpu.make_async_remote_copy(
                src_ref=leaving.at[index, part],
                dst_ref=landed.at[index, part],
                send_sem=red_send.at[index, ring],
                recv_sem=red_recv.at[index, ring],
                device_id=device_at(ring, offset_of(slot)),
                device_id_type=MESH,
            )
            copy.start()
            reduces.append(copy)

    for low, high in ((0, 2), (2, 4), (4, 7)):
        add_cols(low, high, 7)
        for slot in range(2 * low, 2 * high):
            send_back(slot)
    add_rows(7)
    send_back(FAR)
    for copy in reduces:
        copy.wait_recv()
    total = acc[OWN]
    for index in range(RING - 1):
        total = total + landed[index].astype(F32)
    sketch_ref[...] = total

    gram = lax.dot_general(
        total, total, (((0,), (0,)), ((), ())),
        precision=lax.Precision.HIGHEST, preferred_element_type=F32,
    )
    gsrc[...] = gram.reshape(32, 4, SIDE)

    def d1_copy(i):
        other = lax.rem(r + i, 32)
        return pltpu.make_async_remote_copy(
            src_ref=gsrc.at[other],
            dst_ref=g1.at[r],
            send_sem=d1_send.at[i],
            recv_sem=d1_recv.at[r],
            device_id=(other, z),
            device_id_type=MESH,
        )

    def d1_arrival(i):
        other = lax.rem(r + i, 32)
        return pltpu.make_async_remote_copy(
            src_ref=gsrc.at[0],
            dst_ref=g1.at[other],
            send_sem=d1_send.at[i],
            recv_sem=d1_recv.at[other],
            device_id=(other, z),
            device_id_type=MESH,
        )

    each(32, lambda i: d1_copy(i).start())
    g1[r] = gsrc[r]
    each(32, lambda i: d1_arrival(i).wait_recv())
    g2[z] = jnp.sum(g1[...], axis=0)

    def d2_copy(i, mine):
        other = lax.rem(z + i, RING)
        at = z if mine else other
        return pltpu.make_async_remote_copy(
            src_ref=g2.at[at],
            dst_ref=g2.at[at],
            send_sem=d2_send.at[i],
            recv_sem=d2_recv.at[at],
            device_id=(r, other),
            device_id_type=MESH,
        )

    each(RING, lambda i: d2_copy(i, True).start())
    each(RING, lambda i: d2_copy(i, False).wait_recv())
    g3[r] = jnp.sum(g2[...], axis=0)

    def d3_copy(i, mine):
        other = lax.rem(r + i, 32)
        at = r if mine else other
        return pltpu.make_async_remote_copy(
            src_ref=g3.at[at],
            dst_ref=g3.at[at],
            send_sem=d3_send.at[i],
            recv_sem=d3_recv.at[at],
            device_id=(other, z),
            device_id_type=MESH,
        )

    each(32, lambda i: d3_copy(i, True).start())
    each(32, lambda i: d3_copy(i, False).wait_recv())
    gram_ref[...] = g3[...].reshape(SIDE, SIDE) * (1.0 / 65536.0)

    for copy in sent.values():
        copy.wait_send()
    for copy in siblings.values():
        copy.wait_send()
    for copy in reduces:
        copy.wait_send()
    for copy in caux:
        copy.wait_send()
    each(RING, lambda i: raux_copy(i).wait_send())
    each(32, lambda i: d1_copy(i).wait_send())
    each(RING, lambda i: d2_copy(i, True).wait_send())
    each(32, lambda i: d3_copy(i, True).wait_send())


def sketch_and_gram(row_desc, row_scale, col_desc, col_scale, probe, pair_list):
    vmem = pl.BlockSpec(memory_space=pltpu.VMEM)
    hbm = pl.BlockSpec(memory_space=pl.ANY)
    dma = pltpu.SemaphoreType.DMA
    square = jax.ShapeDtypeStruct((SIDE, SIDE), F32)
    return pl.pallas_call(
        sketch_kernel,
        name="sketch_and_gram",
        out_shape=(square, square),
        in_specs=[hbm] * 6,
        out_specs=(vmem, vmem),
        scratch_shapes=[
            pltpu.VMEM((RING, SIDE), F32),
            pltpu.VMEM((RING * SIDE,), BF16),
            pltpu.SMEM((2, 24), jnp.int32),
            pltpu.VMEM((RING, SIDE), F32),
            pltpu.VMEM((RING, SIDE, 1024), BF16),
            pltpu.VMEM((RING, SIDE, 1024 + SIDE), BF16),
            pltpu.VMEM((2, SIDE, 1024), BF16),
            pltpu.VMEM((RING, 2, SIDE), F32),
            pltpu.VMEM((RING, 1, SIDE), F32),
            pltpu.VMEM((2 * RING, SIDE), F32),
            pltpu.VMEM((2 * RING, RING * SIDE), F32),
            pltpu.VMEM((RING * SIDE, SIDE), F32),
            pltpu.VMEM((RING, SIDE, SIDE), F32),
            pltpu.VMEM((RING - 1, SIDE, SIDE), BF16),
            pltpu.VMEM((RING - 1, SIDE, SIDE), BF16),
            pltpu.VMEM((32, 4, SIDE), F32),
            pltpu.VMEM((32, 4, SIDE), F32),
            pltpu.VMEM((RING, 4, SIDE), F32),
            pltpu.VMEM((32, 4, SIDE), F32),
            dma((6,)),
            dma((RINGS, 2, 8, 2)),
            dma((RINGS, 2, 8, 2)),
            dma((8,)),
            dma((8,)),
            dma((RING,)),
            dma((RING,)),
            dma((RING,)),
            dma((RING,)),
            dma((RING - 1, 2)),
            dma((RING - 1, 2)),
            dma((32,)),
            dma((32,)),
            dma((RING,)),
            dma((RING,)),
            dma((32,)),
            dma((32,)),
        ],
        compiler_params=pltpu.CompilerParams(
            collective_id=0, has_side_effects=True, vmem_limit_bytes=56 << 20
        ),
    )(
        row_desc,
        row_scale.reshape(RING, SIDE),
        col_desc,
        col_scale,
        probe,
        pair_list,
    )


def factor_kernel(sketch_ref, gram_ref, basis_ref, factor_ref, work):
    work[:, :SIDE] = gram_ref[...]
    work[:, SIDE:] = sketch_ref[...].T
    for base in range(0, SIDE, PANEL):
        rows = [work[base + i : base + i + 1, :] for i in range(PANEL)]
        low = [
            [jnp.broadcast_to(rows[i][:, base + j : base + j + 1], (1, SIDE)) for j in range(i + 1)]
            for i in range(PANEL)
        ]
        root = []
        for j in range(PANEL):
            root.append(lax.rsqrt(low[j][j]))
            for i in range(j + 1, PANEL):
                low[i][j] = low[i][j] * root[j]
            for i in range(j + 1, PANEL):
                for k in range(j + 1, i + 1):
                    low[i][k] = low[i][k] - low[i][j] * low[k][j]
        left, right = [], []
        for i in range(PANEL):
            a, b = rows[i][:, :SIDE], rows[i][:, SIDE:]
            for j in range(i):
                a = a - low[i][j] * left[j]
                b = b - low[i][j] * right[j]
            left.append(a * root[i])
            right.append(b * root[i])
        work[base : base + PANEL, :SIDE] = jnp.concatenate(left, axis=0)
        work[base : base + PANEL, SIDE:] = jnp.concatenate(right, axis=0)
        rest = base + PANEL
        if rest < SIDE:
            panel = work[base : base + PANEL, :]
            work[rest:, :] = work[rest:, :] - lax.dot_general(
                panel[:, :SIDE], panel, (((0,), (0,)), ((), ())),
                precision=lax.Precision.HIGHEST, preferred_element_type=F32,
            )[rest:, :]
    upper = lax.broadcasted_iota(jnp.int32, (SIDE, SIDE), 1) >= lax.broadcasted_iota(
        jnp.int32, (SIDE, SIDE), 0
    )
    factor_ref[...] = jnp.where(upper, work[:, :SIDE], 0.0)
    basis_ref[...] = work[:, SIDE:].T


def factor_and_solve(sketch, gram):
    vmem = pl.BlockSpec(memory_space=pltpu.VMEM)
    square = jax.ShapeDtypeStruct((SIDE, SIDE), F32)
    return pl.pallas_call(
        factor_kernel,
        name="factor_and_solve",
        out_shape=(square, square),
        in_specs=[vmem, vmem],
        out_specs=(vmem, vmem),
        scratch_shapes=[pltpu.VMEM((SIDE, 2 * SIDE), F32)],
    )(sketch, gram)


def shards(row_desc, row_scale, col_desc, col_scale, probe, pair_list):
    sketch, gram = sketch_and_gram(row_desc, row_scale, col_desc, col_scale, probe, pair_list)
    return factor_and_solve(sketch, gram)


def solution(mesh):
    return jax.shard_map(
        shards,
        mesh=mesh,
        in_specs=(
            P(("row", "col"), None),
            P("row"),
            P("col", None),
            P("col"),
            P("col", None),
            P("row", None),
        ),
        out_specs=(P(("row", "col"), None), P()),
        check_vma=False,
    )
```

```python
import functools

import jax
import jax.numpy as jnp
from jax import lax
from jax.experimental import pallas as pl
from jax.experimental.pallas import tpu as pltpu
from jax.sharding import PartitionSpec as P


RING = 16
OWN, FAR = 14, 15
SIDE = 128
HALF = 64
QUARTER = 32
PANEL = 16
MESH = pl.DeviceIdType.MESH
LOG2E = 1.4426950408889634
F32 = jnp.float32
BF16 = jnp.bfloat16
RINGS = 3


def offset_of(slot):
    if slot == OWN:
        return 0
    if slot == FAR:
        return 8
    distance = slot // 2 + 1
    return -distance if slot % 2 == 0 else distance


def slot_of_offset(offset):
    offset %= RING
    if offset == 0:
        return OWN
    if offset == 8:
        return FAR
    return 2 * (RING - offset - 1) if offset > 8 else 2 * (offset - 1) + 1


def unit_rows(block):
    wide = block.astype(F32)
    total = jnp.sum(wide * wide, axis=1, keepdims=True)
    return (wide * lax.rsqrt(total + 1e-06)).astype(BF16)


def sketch_kernel(
    row_hbm, rscale_hbm, col_hbm, cscale_hbm, probe_hbm, pair_hbm,
    sketch_ref, gram_ref,
    rscale, cscale, pairs, wide, rows, cols, stage, raux, bvec, mstack, cmat, ascale, acc, leaving, landed, gsrc, g1, g2, g3,
    local_sem, ring_send, ring_recv, sib_send, sib_recv, raux_send, raux_recv, caux_send, caux_recv,
    red_send, red_recv, d1_send, d1_recv, d2_send, d2_recv, d3_send, d3_recv,
):
    r = lax.axis_index("row")
    z = lax.axis_index("col")
    core = lax.rem(r, 2)
    p = r // 2
    x = p // 4
    y = lax.rem(p, 4)
    diag = lax.rem(x + y, 4)
    pos = (4 * x + diag, 4 * y + diag)

    def chip_at(ring, place):
        place = lax.rem(place + 2 * RING, RING)
        a = place // 4
        b = lax.rem(place - a + 8, 4)
        return 4 * a + b if ring == 0 else 4 * b + a

    def device_at(ring, offset):
        if ring == 2:
            return (r, lax.rem(z + offset + RING, RING))
        return (2 * chip_at(ring, pos[ring] + offset) + core, z)

    sibling = (2 * p + 1 - core, z)

    barrier = pltpu.get_barrier_semaphore()

    def greet_plane(i, carry):
        pl.semaphore_signal(
            barrier, inc=1, device_id=(lax.rem(r + i, 32), z), device_id_type=MESH
        )
        return carry

    def greet_ring(i, carry):
        pl.semaphore_signal(
            barrier, inc=1, device_id=(r, lax.rem(z + i, RING)), device_id_type=MESH
        )
        return carry

    start = pl.multiple_of(p * SIDE, SIDE)
    own = [
        (row_hbm, stage.at[0]),
        (col_hbm.at[pl.ds(start, SIDE)], stage.at[1]),
        (rscale_hbm, rscale),
        (cscale_hbm, cscale),
        (pair_hbm, pairs),
        (probe_hbm.at[pl.ds(start, SIDE)], cols.at[OWN, :, pl.ds(1024, SIDE)]),
    ]
    own = [pltpu.make_async_copy(a, b, local_sem.at[i]) for i, (a, b) in enumerate(own)]
    for copy in own:
        copy.start()
    lax.fori_loop(1, 32, greet_plane, 0)
    lax.fori_loop(1, RING, greet_ring, 0)
    own[0].wait()
    rows[OWN] = unit_rows(stage[0])
    own[1].wait()
    cols[OWN, :, :1024] = unit_rows(stage[1])
    for copy in own[2:]:
        copy.wait()
    lane = lax.broadcasted_iota(jnp.int32, (1, SIDE), 1)
    block_row = z // 8
    mask = jnp.zeros((1, SIDE), F32)
    for s in range(pairs.shape[1]):
        mask = jnp.where(lane == pairs[block_row, s], 1.0, mask)
    raux[p, 0:1, :] = (2.0 * LOG2E) / rscale[pl.ds(z, 1), :]
    raux[p, 1:2, :] = mask
    wide[...] = cscale[...].astype(F32).reshape(RING, SIDE)
    bvec[OWN] = 1.0 / wide[pl.ds(p, 1), :]
    pl.semaphore_wait(barrier, 46)

    half = pl.ds(pl.multiple_of(core * HALF, HALF), HALF)

    def ring_copy(ring, way, step, sub):
        source = OWN if step == 1 else 2 * (step - 2) + way
        target = FAR if step == 8 else 2 * (step - 1) + way
        low = sub * QUARTER
        if ring == 2:
            part = pl.ds(pl.multiple_of(core * HALF + low, QUARTER), QUARTER)
            buffer = cols
        else:
            part = pl.ds(ring * HALF + low, QUARTER)
            buffer = rows
        return pltpu.make_async_remote_copy(
            src_ref=buffer.at[source, part],
            dst_ref=buffer.at[target, part],
            send_sem=ring_send.at[ring, way, step - 1, sub],
            recv_sem=ring_recv.at[ring, way, step - 1, sub],
            device_id=device_at(ring, 1 - 2 * way),
            device_id_type=MESH,
        )

    def sibling_copy(step):
        first, count = (2 * (step - 1), 2) if step < 8 else (FAR, 1)
        return pltpu.make_async_remote_copy(
            src_ref=cols.at[pl.ds(first, count), half],
            dst_ref=cols.at[pl.ds(first, count), half],
            send_sem=sib_send.at[step - 1],
            recv_sem=sib_recv.at[step - 1],
            device_id=sibling,
            device_id_type=MESH,
        )

    sent = {}

    def pass_on(ring, way, step, sub):
        if step < 8 or sub == way:
            sent[ring, way, step, sub] = ring_copy(ring, way, step, sub)
            sent[ring, way, step, sub].start()

    for sub in range(2):
        for ring in range(RINGS):
            for way in range(2):
                pass_on(ring, way, 1, sub)

    def raux_copy(i):
        other = lax.rem(p + i, RING)
        return pltpu.make_async_remote_copy(
            src_ref=raux.at[p],
            dst_ref=raux.at[p],
            send_sem=raux_send.at[i],
            recv_sem=raux_recv.at[p],
            device_id=(2 * other + core, z),
            device_id_type=MESH,
        )

    def raux_arrival(i):
        other = lax.rem(p + i, RING)
        return pltpu.make_async_remote_copy(
            src_ref=raux.at[other],
            dst_ref=raux.at[other],
            send_sem=raux_send.at[i],
            recv_sem=raux_recv.at[other],
            device_id=(2 * other + core, z),
            device_id_type=MESH,
        )

    def caux_copy(offset):
        target = slot_of_offset(-offset)
        return pltpu.make_async_remote_copy(
            src_ref=bvec.at[OWN],
            dst_ref=bvec.at[target],
            send_sem=caux_send.at[target],
            recv_sem=caux_recv.at[target],
            device_id=device_at(2, offset),
            device_id_type=MESH,
        )

    def each(count, act):
        def body(i, carry):
            act(i)
            return carry

        lax.fori_loop(1, count, body, 0)

    each(RING, lambda i: raux_copy(i).start())
    caux = [caux_copy(offset) for offset in range(1, RING)]
    for copy in caux:
        copy.start()

    def prepare():
        each(RING, lambda i: raux_arrival(i).wait_recv())
        for copy in caux:
            copy.wait_recv()
        eye = lax.broadcasted_iota(jnp.int32, (SIDE, SIDE), 0) == lax.broadcasted_iota(
            jnp.int32, (SIDE, SIDE), 1
        )
        for slot in range(RING):
            first = raux[chip_at(0, pos[0] + offset_of(slot))]
            second = raux[chip_at(1, pos[1] + offset_of(slot))]
            mstack[2 * slot : 2 * slot + 1, :] = first[1:2]
            mstack[2 * slot + 1 : 2 * slot + 2, :] = second[1:2]
            scale = jnp.where(lane < HALF, first[0:1], second[0:1])
            column = jnp.sum(jnp.where(eye, scale, 0.0), axis=1, keepdims=True)
            ascale[slot * SIDE : (slot + 1) * SIDE, :] = jnp.broadcast_to(column, (SIDE, SIDE))
        width = RING * SIDE
        slot_at = lax.broadcasted_iota(jnp.int32, (SIDE, width), 1) // SIDE
        step_at = slot_at // 2 + 1
        shift = jnp.where(slot_at == 2 * (step_at - 1), -step_at, step_at)
        shift = jnp.where(slot_at == OWN, 0, shift)
        shift = jnp.where(slot_at == FAR, 8, shift)
        plane_at = (shift + z + RING) & (RING - 1)
        wanted = lax.broadcasted_iota(jnp.int32, (SIDE, width), 0) == 2 * plane_at + p // 8
        chosen = jnp.dot(
            mstack[...].astype(BF16), wanted.astype(F32).astype(BF16), preferred_element_type=F32
        )
        cmat[...] = (1.0 - chosen) * 1e30 + 1.0

    def tile(r0, m, c0, n):
        lhs = rows[r0 : r0 + m].reshape(m * SIDE, 1024)
        rhs = cols[c0 : c0 + n, :, :1024].reshape(n * SIDE, 1024)
        cosine = lax.dot_general(
            lhs, rhs, (((1,), (1,)), ((), ())), preferred_element_type=F32
        )
        inverse = jnp.concatenate([bvec[c] for c in range(c0, c0 + n)], axis=1)
        parts = []
        for piece in range(2 * m):
            at = 2 * r0 + piece
            shifted = (
                cosine[piece * HALF : (piece + 1) * HALF]
                - cmat[at : at + 1, c0 * SIDE : (c0 + n) * SIDE]
            )
            power = shifted * inverse * ascale[at * HALF : (at + 1) * HALF, :1]
            parts.append(jnp.exp2(power).astype(BF16))
        affinity = jnp.concatenate(parts, axis=0)
        probes = cols[c0 : c0 + n, :, 1024:].reshape(n * SIDE, SIDE)
        return jnp.dot(affinity, probes, preferred_element_type=F32).reshape(m, SIDE, SIDE)

    def add_rows(q):
        acc[2 * q : 2 * q + 2] = tile(2 * q, 2, 0, 2 * q + 2)

    def add_cols(low, high, q):
        if high > low:
            span = slice(2 * low, 2 * high)
            acc[span] = acc[span] + tile(2 * low, 2 * (high - low), 2 * q, 2)

    def take(step, sub):
        for ring in range(RINGS):
            for way in range(2):
                if (ring, way, step, sub) in sent:
                    sent[ring, way, step, sub].wait_recv()
                    if step < 8:
                        pass_on(ring, way, step + 1, sub)

    siblings = {}
    for step in range(1, 9):
        take(step, 0)
        if step >= 3:
            siblings[step - 1].wait_recv()
            if step == 3:
                add_rows(0)
            add_rows(step - 2)
        take(step, 1)
        siblings[step] = sibling_copy(step)
        siblings[step].start()
        if step == 2:
            siblings[1].wait_recv()
            prepare()
        if step >= 3:
            add_cols(0, step - 2, step - 2)
    siblings[8].wait_recv()

    reduces = []

    def send_back(slot):
        index = slot if slot < OWN else OWN
        leaving[index] = acc[slot].astype(BF16)
        for ring in range(2):
            part = pl.ds(ring * HALF, HALF)
            copy = pltpu.make_async_remote_copy(
                src_ref=leaving.at[index, part],
                dst_ref=landed.at[index, part],
                send_sem=red_send.at[index, ring],
                recv_sem=red_recv.at[index, ring],
                device_id=device_at(ring, offset_of(slot)),
                device_id_type=MESH,
            )
            copy.start()
            reduces.append(copy)

    for low, high in ((0, 2), (2, 4), (4, 7)):
        add_cols(low, high, 7)
        for slot in range(2 * low, 2 * high):
            send_back(slot)
    add_rows(7)
    send_back(FAR)
    for copy in [*sent.values(), *siblings.values(), *caux]:
        copy.wait_send()
    each(RING, lambda i: raux_copy(i).wait_send())
    total = acc[OWN]
    for index in range(RING - 1):
        for copy in reduces[2 * index : 2 * index + 2]:
            copy.wait_recv()
        total = total + landed[index].astype(F32)
    sketch_ref[...] = total

    gram = lax.dot_general(
        total, total, (((0,), (0,)), ((), ())),
        precision=lax.Precision.HIGHEST, preferred_element_type=F32,
    )
    gsrc[...] = gram.reshape(32, 4, SIDE)

    def d1_copy(i):
        other = lax.rem(r + i, 32)
        return pltpu.make_async_remote_copy(
            src_ref=gsrc.at[other],
            dst_ref=g1.at[r],
            send_sem=d1_send.at[i],
            recv_sem=d1_recv.at[r],
            device_id=(other, z),
            device_id_type=MESH,
        )

    def d1_arrival(i):
        other = lax.rem(r + i, 32)
        return pltpu.make_async_remote_copy(
            src_ref=gsrc.at[0],
            dst_ref=g1.at[other],
            send_sem=d1_send.at[i],
            recv_sem=d1_recv.at[other],
            device_id=(other, z),
            device_id_type=MESH,
        )

    each(32, lambda i: d1_copy(i).start())
    for copy in reduces:
        copy.wait_send()
    g1[r] = gsrc[r]
    each(32, lambda i: d1_arrival(i).wait_recv())
    g2[z] = jnp.sum(g1[...], axis=0)

    def d2_copy(i, mine):
        other = lax.rem(z + i, RING)
        at = z if mine else other
        return pltpu.make_async_remote_copy(
            src_ref=g2.at[at],
            dst_ref=g2.at[at],
            send_sem=d2_send.at[i],
            recv_sem=d2_recv.at[at],
            device_id=(r, other),
            device_id_type=MESH,
        )

    each(RING, lambda i: d2_copy(i, True).start())
    each(32, lambda i: d1_copy(i).wait_send())
    each(RING, lambda i: d2_copy(i, False).wait_recv())
    g3[r] = jnp.sum(g2[...], axis=0)

    def d3_copy(i, mine):
        other = lax.rem(r + i, 32)
        at = r if mine else other
        return pltpu.make_async_remote_copy(
            src_ref=g3.at[at],
            dst_ref=g3.at[at],
            send_sem=d3_send.at[i],
            recv_sem=d3_recv.at[at],
            device_id=(other, z),
            device_id_type=MESH,
        )

    each(32, lambda i: d3_copy(i, True).start())
    each(RING, lambda i: d2_copy(i, True).wait_send())
    each(32, lambda i: d3_copy(i, False).wait_recv())
    gram_ref[...] = g3[...].reshape(SIDE, SIDE) * (1.0 / 65536.0)

    each(32, lambda i: d3_copy(i, True).wait_send())


def sketch_and_gram(row_desc, row_scale, col_desc, col_scale, probe, pair_list):
    vmem = pl.BlockSpec(memory_space=pltpu.VMEM)
    hbm = pl.BlockSpec(memory_space=pl.ANY)
    dma = pltpu.SemaphoreType.DMA
    square = jax.ShapeDtypeStruct((SIDE, SIDE), F32)
    return pl.pallas_call(
        sketch_kernel,
        name="sketch_and_gram",
        out_shape=(square, square),
        in_specs=[hbm] * 6,
        out_specs=(vmem, vmem),
        scratch_shapes=[
            pltpu.VMEM((RING, SIDE), F32),
            pltpu.VMEM((RING * SIDE,), BF16),
            pltpu.SMEM((2, 24), jnp.int32),
            pltpu.VMEM((RING, SIDE), F32),
            pltpu.VMEM((RING, SIDE, 1024), BF16),
            pltpu.VMEM((RING, SIDE, 1024 + SIDE), BF16),
            pltpu.VMEM((2, SIDE, 1024), BF16),
            pltpu.VMEM((RING, 2, SIDE), F32),
            pltpu.VMEM((RING, 1, SIDE), F32),
            pltpu.VMEM((2 * RING, SIDE), F32),
            pltpu.VMEM((2 * RING, RING * SIDE), F32),
            pltpu.VMEM((RING * SIDE, SIDE), F32),
            pltpu.VMEM((RING, SIDE, SIDE), F32),
            pltpu.VMEM((RING - 1, SIDE, SIDE), BF16),
            pltpu.VMEM((RING - 1, SIDE, SIDE), BF16),
            pltpu.VMEM((32, 4, SIDE), F32),
            pltpu.VMEM((32, 4, SIDE), F32),
            pltpu.VMEM((RING, 4, SIDE), F32),
            pltpu.VMEM((32, 4, SIDE), F32),
            dma((6,)),
            dma((RINGS, 2, 8, 2)),
            dma((RINGS, 2, 8, 2)),
            dma((8,)),
            dma((8,)),
            dma((RING,)),
            dma((RING,)),
            dma((RING,)),
            dma((RING,)),
            dma((RING - 1, 2)),
            dma((RING - 1, 2)),
            dma((32,)),
            dma((32,)),
            dma((RING,)),
            dma((RING,)),
            dma((32,)),
            dma((32,)),
        ],
        compiler_params=pltpu.CompilerParams(
            collective_id=0, has_side_effects=True, vmem_limit_bytes=56 << 20
        ),
    )(
        row_desc,
        row_scale.reshape(RING, SIDE),
        col_desc,
        col_scale,
        probe,
        pair_list,
    )


def factor_kernel(sketch_ref, gram_ref, basis_ref, factor_ref, work):
    work[:, :SIDE] = gram_ref[...]
    work[:, SIDE:] = sketch_ref[...].T
    for base in range(0, SIDE, PANEL):
        rows = [work[base + i : base + i + 1, :] for i in range(PANEL)]
        low = [
            [jnp.broadcast_to(rows[i][:, base + j : base + j + 1], (1, SIDE)) for j in range(i + 1)]
            for i in range(PANEL)
        ]
        root = []
        for j in range(PANEL):
            root.append(lax.rsqrt(low[j][j]))
            for i in range(j + 1, PANEL):
                low[i][j] = low[i][j] * root[j]
            for i in range(j + 1, PANEL):
                for k in range(j + 1, i + 1):
                    low[i][k] = low[i][k] - low[i][j] * low[k][j]
        left, right = [], []
        for i in range(PANEL):
            a, b = rows[i][:, :SIDE], rows[i][:, SIDE:]
            for j in range(i):
                a = a - low[i][j] * left[j]
                b = b - low[i][j] * right[j]
            left.append(a * root[i])
            right.append(b * root[i])
        work[base : base + PANEL, :SIDE] = jnp.concatenate(left, axis=0)
        work[base : base + PANEL, SIDE:] = jnp.concatenate(right, axis=0)
        rest = base + PANEL
        if rest < SIDE:
            panel = work[base : base + PANEL, :]
            work[rest:, :] = work[rest:, :] - lax.dot_general(
                panel[:, :SIDE], panel, (((0,), (0,)), ((), ())),
                precision=lax.Precision.HIGHEST, preferred_element_type=F32,
            )[rest:, :]
    upper = lax.broadcasted_iota(jnp.int32, (SIDE, SIDE), 1) >= lax.broadcasted_iota(
        jnp.int32, (SIDE, SIDE), 0
    )
    factor_ref[...] = jnp.where(upper, work[:, :SIDE], 0.0)
    basis_ref[...] = work[:, SIDE:].T


def factor_and_solve(sketch, gram):
    vmem = pl.BlockSpec(memory_space=pltpu.VMEM)
    square = jax.ShapeDtypeStruct((SIDE, SIDE), F32)
    return pl.pallas_call(
        factor_kernel,
        name="factor_and_solve",
        out_shape=(square, square),
        in_specs=[vmem, vmem],
        out_specs=(vmem, vmem),
        scratch_shapes=[pltpu.VMEM((SIDE, 2 * SIDE), F32)],
    )(sketch, gram)


def shards(row_desc, row_scale, col_desc, col_scale, probe, pair_list):
    sketch, gram = sketch_and_gram(row_desc, row_scale, col_desc, col_scale, probe, pair_list)
    return factor_and_solve(sketch, gram)


def solution(mesh):
    return jax.shard_map(
        shards,
        mesh=mesh,
        in_specs=(
            P(("row", "col"), None),
            P("row"),
            P("col", None),
            P("col"),
            P("col", None),
            P("row", None),
        ),
        out_specs=(P(("row", "col"), None), P()),
        check_vma=False,
    )
```
